32 devices in a mesh: dp: 8 (over z, y), head: 2 (over x), ctx: 2 (over core).
Axes of the slice: x: 2, y: 2, z: 4, core: 2. Of those that a mesh axis runs over, the one named last changes fastest.
Arguments:
- tokens: bfloat16 [8, 2, 1024, 768], P('dp', 'ctx', 'head'), may hold values from -6 to 6
- upstream: bfloat16 [8, 2, 1024, 768], P('dp', 'ctx', 'head'), may hold values from -6 to 6
- group_ids: int32 [8], P('dp'), may hold values from 0 to 3
- group_weights: int32 [4], replicated, may hold values from 1 to 4
- norm_gain1: float32 [768], replicated, may hold values from 0.5 to 1.5
- w_qkv: bfloat16 [768, 3, 768], P(None, None, 'head'), may hold values from -0.21875 to 0.21875
- w_gate: bfloat16 [768, 768], P(None, 'head'), may hold values from -0.21875 to 0.21875
- w_rate: bfloat16 [768, 12], P(None, 'head'), may hold values from -0.21875 to 0.21875
- b_rate: float32 [12], P('head'), may hold values from -1 to 1
- w1_init: float32 [12, 64, 256], P('head'), may hold values from -0.75 to 0.75
- c1_init: float32 [12, 256], P('head'), may hold values from -2 to 2
- w2_init: float32 [12, 256, 64], P('head'), may hold values from -0.375 to 0.375
- c2_init: float32 [12, 64], P('head'), may hold values from -2 to 2
- inner_gain: float32 [12, 64], P('head'), may hold values from 0.5 to 1.5
- inner_bias: float32 [12, 64], P('head'), may hold values from -2 to 2
- out_proj: bfloat16 [768, 768], P('head'), may hold values from -0.21875 to 0.21875
- norm_gain2: float32 [768], replicated, may hold values from 0.5 to 1.5
- w_gu: bfloat16 [768, 2, 2048], P(None, None, 'head'), may hold values from -0.21875 to 0.21875
- w_down: bfloat16 [2048, 768], P('head'), may hold values from -0.125 to 0.125
Outputs:
- block_output: bfloat16 [8, 2, 1024, 768], P('dp', 'ctx', 'head')
- x_grad: float32 [8, 2, 1024, 768], P('dp', 'ctx', 'head')
- gain1_grad: float32 [768], replicated
- qkv_grad: float32 [768, 3, 768], P(None, None, 'head')
- gate_grad: float32 [768, 768], P(None, 'head')
- rate_grad: float32 [768, 12], P(None, 'head')
- rate_bias_grad: float32 [12], P('head')
- w1_grad: float32 [12, 64, 256], P('head')
- c1_grad: float32 [12, 256], P('head')
- w2_grad: float32 [12, 256, 64], P('head')
- c2_grad: float32 [12, 64], P('head')
- inner_gain_grad: float32 [12, 64], P('head')
- inner_bias_grad: float32 [12, 64], P('head')
- out_proj_grad: float32 [768, 768], P('head')
- gain2_grad: float32 [768], replicated
- gate_up_grad: float32 [768, 2, 2048], P(None, None, 'head')
- down_grad: float32 [2048, 768], P('head')
The draws below stay inside these ranges and needn't reach their ends.
All inputs are finite; a program needn't handle non-finite values.
Results may differ from the reference program's by a relative error of at most 0.015.
Values may be sent and summed in bfloat16 or wider, within the bound.
No kernel may reach another device: no remote copies, remote signals or barrier semaphores. Data moves between devices by JAX's collectives and lax.ppermute only.
A program may use at most 256 MiB of HBM per device.

```python
import jax
import jax.numpy as jnp
from jax import lax

D = 768
HEADS = 12
HEAD_DIM = 64
INNER = 256
FF = 2048
MB = 16
LENGTH = 2048
GROUPS = 4
SEQS = 8
PIECES = 2
HALF = 1024


def plant(values, rng, low, top_value):
    longest = values.shape.index(max(values.shape))
    spots = []
    for shift in (0, 1):
        where = [jax.random.randint(jax.random.fold_in(rng, axis), (), 0, length) for axis, length in enumerate(values.shape)]
        where[longest] = (where[longest] + shift) % values.shape[longest]
        spots.append(tuple(where))
    return values.at[spots[0]].set(low).at[spots[1]].set(top_value)


def levels(key, extent, shards, smallest, top_value):
    gain, own = 1.0, jax.random.fold_in(key, 6)
    for position, blocks in shards:
        heights = jnp.exp(jax.random.uniform(jax.random.fold_in(own, position), (blocks,), jnp.float32, smallest / len(shards), top_value / len(shards)))
        gain = gain * jnp.repeat(heights, extent[position] // blocks).reshape([-1 if axis == position else 1 for axis in range(len(extent))])
    return gain


def noise(key, shape, spread, bound, shards=(), dtype=jnp.bfloat16):
    entries = jax.random.normal(key, shape, jnp.float32) * spread
    if len(shards) > 0:
        entries = levels(key, shape, shards, -0.22, 0.18) * entries
    return jnp.clip(entries, min=-bound, max=bound).astype(dtype)


def setup_inputs(seed: int = 0) -> dict:
    key_list = jax.random.split(jax.random.key(seed), 20)
    tokens = noise(key_list[0], (SEQS, PIECES, HALF, D), 1.0, 6.0, ((0, 8), (1, 2), (2, 2)))
    upstream = noise(key_list[1], (SEQS, PIECES, HALF, D), 1.0, 6.0, ((0, 8), (1, 2), (2, 2)))
    group_ids = plant(jax.random.randint(key_list[2], (SEQS,), 0, GROUPS), jax.random.fold_in(key_list[2], 1), 0, GROUPS - 1).astype(jnp.int32)
    group_weights = plant(jax.random.randint(key_list[3], (GROUPS,), 1, 5), jax.random.fold_in(key_list[3], 1), 1, 4).astype(jnp.int32)
    norm_gain1 = jnp.clip(1.0 + 0.1 * jax.random.normal(key_list[4], (D,), jnp.float32), 0.5, 1.5)
    w_qkv = noise(key_list[5], (D, 3, D), D ** -0.5, 0.21875, ((2, 2),))
    w_gate = noise(key_list[6], (D, D), D ** -0.5, 0.21875, ((1, 2),))
    w_rate = noise(key_list[7], (D, HEADS), D ** -0.5, 0.21875, ((1, 2),))
    b_rate = jnp.clip(jax.random.uniform(key_list[8], (HEADS,), jnp.float32, -1.0, 1.0) * levels(key_list[8], (HEADS,), ((0, 2),), -0.4, 0.0), -1.0, 1.0)
    w1_init = noise(key_list[9], (HEADS, HEAD_DIM, INNER), HEAD_DIM ** -0.5, 0.75, ((0, 2),), jnp.float32)
    c1_init = noise(key_list[10], (HEADS, INNER), 0.3, 2.0, ((0, 2),), jnp.float32)
    w2_init = noise(key_list[11], (HEADS, INNER, HEAD_DIM), INNER ** -0.5, 0.375, ((0, 2),), jnp.float32)
    c2_init = noise(key_list[12], (HEADS, HEAD_DIM), 0.3, 2.0, ((0, 2),), jnp.float32)
    inner_gain = jnp.clip(1.0 + 0.1 * jax.random.normal(key_list[13], (HEADS, HEAD_DIM), jnp.float32), 0.5, 1.5)
    inner_bias = noise(key_list[14], (HEADS, HEAD_DIM), 0.3, 2.0, ((0, 2),), jnp.float32)
    out_proj = noise(key_list[15], (D, D), D ** -0.5, 0.21875, ((0, 2),))
    norm_gain2 = jnp.clip(1.0 + 0.1 * jax.random.normal(key_list[16], (D,), jnp.float32), 0.5, 1.5)
    w_gu = noise(key_list[17], (D, 2, FF), D ** -0.5, 0.21875, ((2, 2),))
    w_down = noise(key_list[18], (FF, D), FF ** -0.5, 0.125, ((0, 2),))
    return {"tokens": tokens, "upstream": upstream, "group_ids": group_ids, "group_weights": group_weights, "norm_gain1": norm_gain1, "w_qkv": w_qkv, "w_gate": w_gate, "w_rate": w_rate, "b_rate": b_rate, "w1_init": w1_init, "c1_init": c1_init, "w2_init": w2_init, "c2_init": c2_init, "inner_gain": inner_gain, "inner_bias": inner_bias, "out_proj": out_proj, "norm_gain2": norm_gain2, "w_gu": w_gu, "w_down": w_down}


@jax.custom_vjp
def low(v):
    return lax.optimization_barrier(v.astype(jnp.bfloat16)).astype(jnp.float32)

@jax.custom_vjp
def low_back(v):
    return v

def low_keep(v):
    return (low(v), None)

def low_pass(kept, grad):
    return (grad,)

def back_keep(v):
    return (v, None)

def back_low(kept, grad):
    return (low(grad),)
low.defvjp(low_keep, low_pass)
low_back.defvjp(back_keep, back_low)
highest = lax.Precision.HIGHEST
base_rate = 0.3

def gelu_value(values):
    return 0.5 * values * (1.0 + lax.erf(values * 0.7071067811865476))

def gelu_slope(values):
    return 0.5 * (1.0 + lax.erf(values * 0.7071067811865476)) + values * jnp.exp(-0.5 * values * values) * 0.3989422804014327

def rms_gain(values, gains):
    return values * lax.rsqrt(lax.optimization_barrier(jnp.mean(values * values, axis=-1, keepdims=True)) + 1e-06) * gains

def inner_norm(values, gains, biases):
    center = values - lax.optimization_barrier(jnp.mean(values, axis=-1, keepdims=True))
    rscale = lax.rsqrt(lax.optimization_barrier(jnp.mean(center * center, axis=-1, keepdims=True)) + 1e-06)
    z_hat = center * rscale
    return (z_hat * gains + biases, z_hat, rscale)

def contract(pattern, left_op, right_op):
    return jnp.einsum(pattern, left_op, right_op, precision=highest)

def inner_step(carried, inputs, gains, biases):
    w_one, c_one, w_two, c_two = carried
    queries, keyset, values, step_rates = inputs
    gain_rows = gains[:, None, :]
    bias_rows = biases[:, None, :]
    z_one = contract('bmd,bdf->bmf', keyset, w_one) + c_one[:, None, :]
    hidden_key = gelu_value(z_one)
    z_two = contract('bmf,bfd->bmd', hidden_key, w_two) + c_two[:, None, :]
    recon, z_hat, rscale = inner_norm(z_two, gain_rows, bias_rows)
    scaled = (recon - (values - keyset)) * gain_rows
    g_two = rscale * (scaled - lax.optimization_barrier(jnp.mean(scaled, axis=-1, keepdims=True)) - z_hat * lax.optimization_barrier(jnp.mean(scaled * z_hat, axis=-1, keepdims=True)))
    g_one = contract('bmd,bfd->bmf', g_two, w_two) * gelu_slope(z_one)
    mb_size = queries.shape[1]
    causal = (lax.broadcasted_iota(jnp.int32, (mb_size, mb_size), 0) >= lax.broadcasted_iota(jnp.int32, (mb_size, mb_size), 1)).astype(jnp.float32)
    mixing = step_rates[:, None, :] * causal[None, :, :]
    z_query = contract('bmd,bdf->bmf', queries, w_one) + c_one[:, None, :] - contract('bms,bsf->bmf', mixing * (contract('bmd,bsd->bms', queries, keyset) + 1.0), g_one)
    hidden_query = gelu_value(z_query)
    z_out = contract('bmf,bfd->bmd', hidden_query, w_two) + c_two[:, None, :] - contract('bms,bsd->bmd', mixing * (contract('bmf,bsf->bms', hidden_query, hidden_key) + 1.0), g_two)
    normed, _, _ = inner_norm(z_out, gain_rows, bias_rows)
    step_one = g_one * step_rates[:, :, None]
    step_two = g_two * step_rates[:, :, None]
    new_state = (w_one - contract('bmd,bmf->bdf', keyset, step_one), c_one - lax.optimization_barrier(jnp.sum(step_one, axis=1)), w_two - contract('bmf,bmd->bfd', hidden_key, step_two), c_two - lax.optimization_barrier(jnp.sum(step_two, axis=1)))
    return (new_state, queries + normed)

def inner_chain(state_in, queries, keyset, values, logits, gains, biases):
    step_rates = jax.nn.sigmoid(logits) * (base_rate / queries.shape[-1])
    num_blocks = queries.shape[1] // MB

    def blocked(array):
        return jnp.swapaxes(array.reshape((array.shape[0], num_blocks, MB) + array.shape[2:]), 0, 1)

    def advance(carried, inputs):
        return inner_step(carried, inputs, gains, biases)
    final_state, produced = lax.scan(jax.checkpoint(advance), state_in, (blocked(queries), blocked(keyset), blocked(values), blocked(step_rates)))
    return (final_state, jnp.swapaxes(produced, 0, 1).reshape(queries.shape))

def block(x_seq, gain_one, w_qkv, w_gate, w_rate, b_rate, w1_init, c1_init, w2_init, c2_init, inner_gain, inner_bias, out_proj, gain_two, w_gu, w_down):
    length_here = x_seq.shape[0]
    normed_one = low(rms_gain(x_seq, gain_one))
    qkv_all = low(low_back(jnp.dot(normed_one, w_qkv.reshape(D, 3 * D), precision=highest))).reshape(length_here, 3, HEADS, HEAD_DIM)
    gate_pre = low_back(jnp.dot(normed_one, w_gate, precision=highest))
    logits = low_back(jnp.dot(normed_one, w_rate, precision=highest) + b_rate)
    heads_first = jnp.transpose(qkv_all, (1, 2, 0, 3))
    _, produced = inner_chain((w1_init, c1_init, w2_init, c2_init), heads_first[0], heads_first[1], heads_first[2], logits.T, inner_gain, inner_bias)
    ttt_out = jnp.transpose(produced, (1, 0, 2)).reshape(length_here, D)
    gated = low(gelu_value(gate_pre) * ttt_out)
    middle = x_seq + low_back(jnp.dot(gated, out_proj, precision=highest))
    normed_two = low(rms_gain(middle, gain_two))
    gate_up = low_back(jnp.dot(normed_two, w_gu.reshape(D, 2 * FF), precision=highest)).reshape(length_here, 2, FF)
    hidden = low(jax.nn.silu(gate_up[:, 0]) * gate_up[:, 1])
    return middle + low_back(jnp.dot(hidden, w_down, precision=highest))

def reference(tokens, upstream, group_ids, group_weights, norm_gain1, w_qkv, w_gate, w_rate, b_rate, w1_init, c1_init, w2_init, c2_init, inner_gain, inner_bias, out_proj, norm_gain2, w_gu, w_down):
    params = tuple((param.astype(jnp.float32) for param in (norm_gain1, w_qkv, w_gate, w_rate, b_rate, w1_init, c1_init, w2_init, c2_init, inner_gain, inner_bias, out_proj, norm_gain2, w_gu, w_down)))
    x_all = tokens.astype(jnp.float32).reshape(SEQS, LENGTH, D)
    cot_all = upstream.astype(jnp.float32).reshape(SEQS, LENGTH, D)
    scales = group_weights[group_ids].astype(jnp.float32)

    def one_sequence(totals, inputs):
        x_seq, cot_seq, scale_one = inputs
        output, pullback = jax.vjp(block, x_seq, *params)
        grads = pullback(cot_seq * scale_one)
        return (tuple((total + grad for total, grad in zip(totals, grads[1:]))), (output.astype(jnp.bfloat16), grads[0]))
    starts = tuple((jnp.zeros_like(param) for param in params))
    totals, (outputs, x_grads) = lax.scan(one_sequence, starts, (x_all, cot_all, scales))
    out_shape = (SEQS, PIECES, HALF, D)
    return (outputs.reshape(out_shape), x_grads.reshape(out_shape), totals[0], totals[1], totals[2], totals[3], totals[4], totals[5], totals[6], totals[7], totals[8], totals[9], totals[10], totals[11], totals[12], totals[13], totals[14])
```

```python
import functools
import jax, jax.numpy as jnp
from jax import lax
from jax.experimental import pallas as pl
from jax.experimental.pallas import tpu as pltpu
from jax.sharding import PartitionSpec as P

MB = 16
CHUNK = 256
base_rate = 0.3
BODY = 256
TILE = 128
WIDE = 128
SPAN = 128
VMEM_BYTES = 56 * 2**20
f32, bf16 = jnp.float32, jnp.bfloat16


def dot(a, b, ca, cb):
    return lax.dot_general(a.astype(bf16), b.astype(bf16), (((ca,), (cb,)), ((), ())), preferred_element_type=f32)


def nn(a, b):
    return dot(a, b, 1, 0)


def nt(a, b):
    return dot(a, b, 1, 1)


def tn(a, b):
    return dot(a, b, 0, 0)


def rows(x):
    return jnp.sum(x, axis=-1, keepdims=True)


def normal_parts(v):
    return 0.5 + 0.5 * lax.erf(v * 0.7071067811865476), jnp.exp(-0.5 * v * v) * 0.3989422804014327


def rate_of(logits, hd):
    return jax.nn.sigmoid(logits) * (base_rate / hd)


def fwd_kernel(nh, order_ref, r0_ref, r1_ref, r2_ref, r3_ref, gain_ref, wp_ref, ww_ref, bw_ref, wt_ref, bt_ref, w1_ref, c1_ref, w2_ref, c2_ref, g_ref, b_ref,
               p0_ref, p1_ref, p2_ref, p3_ref, out_ref, gate_ref, norm_ref, qkv_ref, eb_ref, etar_ref, a_ref, gp_ref, hg_ref, g1_ref, g2_ref, w2all_ref, w1c_ref, c1c_ref, c2c_ref,
               zh_ref, eg_ref, va_ref, vb_ref, vd_ref, vr_ref, bq_ref, gq_ref, ph_ref, rp_ref,
               w1_s, w2_s, c1_s, c2_s, k_s, q_s, t_s, pre_s, cur_s, eg1_s, proj_s, x_s, tm_s):
    hd = w1_s.shape[1]
    C = qkv_ref.shape[0]
    inner = w1_s.shape[2]
    H = range(nh)
    inv = 1.0 / hd
    bodies = C // BODY
    steps = BODY // MB

    @pl.when(pl.program_id(0) == 0)
    def _():
        w1_s[...] = w1_ref[...]
        w2_s[...] = w2_ref[...]
        c1_s[...] = c1_ref[...]
        c2_s[...] = c2_ref[...]

    which = order_ref[4, pl.program_id(0)]
    for p, ref in enumerate((r0_ref, r1_ref, r2_ref, r3_ref)):
        @pl.when(which == p)
        def _(ref=ref):
            x_s[...] = ref[...]

    for i in range(0, C, BODY):
        x = x_s[i:i + BODY, :].astype(f32)
        scale = lax.rsqrt(rows(x * x) * (1.0 / x.shape[1]) + 1e-6)
        norm_ref[i:i + BODY, :] = (x * scale * gain_ref[...]).astype(bf16)
    normed = norm_ref[...]
    proj_s[...] = nn(normed, wp_ref[...])
    qkv_ref[...] = proj_s[:, :3 * nh * hd].astype(bf16)
    gate_ref[...] = proj_s[:, 3 * nh * hd:]
    wide = nn(normed, ww_ref[...]) + bw_ref[...]
    for h in H:
        eb_ref[h] = rate_of(wide[:, h * 128:(h + 1) * 128], hd)
    etar_ref[...] = rate_of(nt(wt_ref[...], normed) + bt_ref[:, :1], hd)

    for h in H:
        k = qkv_ref[:, (nh + h) * hd:(nh + h + 1) * hd]
        v = qkv_ref[:, (2 * nh + h) * hd:(2 * nh + h + 1) * hd]
        k_s[h] = k
        q_s[h] = qkv_ref[:, h * hd:(h + 1) * hd]
        w1b = w1_s[h].astype(bf16)
        w1c_ref[0, h] = w1b
        c1c_ref[0, h] = c1_s[h]
        c2c_ref[0, h] = c2_s[h]
        pre_s[h] = nn(k, w1b) + c1_s[h]
        t = (b_ref[h] - v.astype(f32) + k.astype(f32)) * g_ref[h]
        mean = jnp.broadcast_to(rows(t) * inv, t.shape)
        t_s[h] = t - mean
        tm_s[h] = mean

    g2 = [g_ref[h] * g_ref[h] for h in H]
    g2m = [rows(g2[h]) * inv for h in H]
    w2 = [w2_s[h] for h in H]
    c2 = [c2_s[h] for h in H]
    csum = [0.0 for h in H]

    for j in range(bodies):
        lo, hi = j * BODY, (j + 1) * BODY
        kb = [k_s[h, lo:hi, :] for h in H]
        mix = [(nt(kb[h], kb[h]) + 1.0).astype(bf16) for h in H]
        for h in H:
            if j > 0:
                past = (nt(kb[h], k_s[h, :lo, :]) + 1.0).astype(bf16)
                cur_s[h] = pre_s[h, lo:hi, :] - nn(past, eg1_s[h, :lo, :])
            else:
                cur_s[h] = pre_s[h, lo:hi, :]
        eg1 = [[] for h in H]
        outs = []
        for u in range(steps):
            i = j * steps + u
            sl = slice(i * MB, (i + 1) * MB)
            e = [eb_ref[h, sl, :] for h in H]
            e2 = [jnp.concatenate([e[h]] * (inner // 128), axis=1) for h in H]
            e1 = [e[h][:, :hd] for h in H]
            w2b = [w2[h].astype(bf16) for h in H]
            z1 = [cur_s[h, u * MB:(u + 1) * MB, :] for h in H]
            if u > 0:
                z1 = [z1[h] - nn(mix[h][u * MB:(u + 1) * MB, :u * MB], jnp.concatenate(eg1[h], axis=0)) for h in H]
            Ht = [nn(t_s[h, sl, :], w2b[h]) for h in H]
            a, gp, gpp = [], [], []
            for h in H:
                cdf, bell = normal_parts(z1[h])
                a.append((z1[h] * cdf).astype(bf16))
                gp.append(cdf + z1[h] * bell)
                gpp.append(bell * (2.0 - z1[h] * z1[h]))
            z2 = [nt(a[h], w2b[h]) + c2[h] for h in H]
            zb = [jnp.concatenate([z2[h] * g2[h], z2[h]], axis=0).astype(bf16) for h in H]
            Hz = [nn(zb[h], w2b[h]) for h in H]
            G2, Hh, wl, wr = [], [], [], []
            for h in H:
                z, t = z2[h], t_s[h, sl, :]
                gz = g2[h] * z
                mu = rows(z) * inv
                zz = rows(z * z) * inv
                s1 = rows(gz) * inv
                s2 = rows(gz * z) * inv
                s3 = rows(t * z) * inv
                r = lax.rsqrt(zz - mu * mu + 1e-6)
                rr = r * r
                zh = (z - mu) * r
                q1 = r * (s1 - mu * g2m[h])
                q2 = rr * (s2 - 2.0 * mu * s1 + mu * mu * g2m[h])
                m2 = q2 + r * s3
                gap = g2[h] - m2
                G2.append(r * (zh * gap + t - q1))
                af, ee = a[h].astype(f32), e2[h]
                wl.append(jnp.concatenate([zb[h], t.astype(bf16), jnp.ones_like(t).astype(bf16)], axis=0))
                wr.append(jnp.concatenate([(ee * rr) * af, -(ee * (rr * m2)) * af, (ee * r) * af, (ee * (rr * (m2 * mu - s1))) * af], axis=0).astype(bf16))
                Hh.append(rr * Hz[h][:MB] - (rr * m2) * Hz[h][MB:] + r * Ht[h])
                Eg = 2.0 * (g2[h] * zh) + t
                zh_ref[h, sl, :] = zh
                eg_ref[h, sl, :] = Eg + tm_s[h, sl, :]
                va_ref[h, sl, :] = rr * gap
                vb_ref[h, sl, :] = rr * (Eg - 2.0 * q1 - (3.0 * m2 + q2) * zh)
                vd_ref[h, sl, :] = rr * zh
                vr_ref[h, sl, :] = jnp.broadcast_to(r, zh.shape)
            G2b = [G2[h].astype(bf16) for h in H]
            G1 = [Hh[h] * gp[h] for h in H]
            eG1 = [e2[h] * G1[h] for h in H]
            eG2 = [(e1[h] * G2[h]).astype(bf16) for h in H]
            for h in H:
                b = eG1[h].astype(bf16)
                eg1[h].append(b)
                eg1_s[h, sl, :] = b
                csum[h] = csum[h] + eG1[h]
                a_ref[h, sl, :] = a[h]
                gp_ref[h, sl, :] = gp[h].astype(bf16)
                hg_ref[h, sl, :] = (Hh[h] * gpp[h]).astype(bf16)
                g1_ref[h, sl, :] = G1[h].astype(bf16)
                g2_ref[h, sl, :] = G2b[h]
                w2all_ref[i, h] = w2b[h]
                w2[h] = w2[h] - tn(wl[h], wr[h])
                c2[h] = c2[h] - jnp.sum(eG2[h].astype(f32), axis=0, keepdims=True)
    for h in H:
        w2_s[h] = w2[h]
        c2_s[h] = c2[h]
        w1_s[h] = w1_s[h] - tn(k_s[h], eg1_s[h])
        c1_s[h] = c1_s[h] - jnp.sum(csum[h], axis=0, keepdims=True)

    for lo in range(0, C, TILE):
        hi = lo + TILE
        tri = lax.broadcasted_iota(jnp.int32, (TILE, hi), 0) + lo >= lax.broadcasted_iota(jnp.int32, (TILE, hi), 1)
        q = [q_s[h, lo:hi, :] for h in H]
        M = [jnp.where(tri, etar_ref[h:h + 1, :hi], 0.0) for h in H]
        N1 = [(M[h] * (nt(q[h], k_s[h, :hi, :]) + 1.0)).astype(bf16) for h in H]
        p1 = [nn(q[h], w1c_ref[0, h]) + c1c_ref[0, h] - nn(N1[h], g1_ref[h, :hi, :]) for h in H]
        B = []
        for h in H:
            cdf, bell = normal_parts(p1[h])
            B.append((p1[h] * cdf).astype(bf16))
            bq_ref[h, lo:hi, :] = B[h]
            gq_ref[h, lo:hi, :] = (cdf + p1[h] * bell).astype(bf16)
        N2 = [(M[h] * (nt(B[h], a_ref[h, :hi, :]) + 1.0)).astype(bf16) for h in H]
        p2 = [nt(B[h], w2all_ref[0, h]) + c2c_ref[0, h] - nn(N2[h], g2_ref[h, :hi, :]) for h in H]
        outs = []
        for h in H:
            c = p2[h] - rows(p2[h]) * inv
            r = lax.rsqrt(rows(c * c) * inv + 1e-6)
            ph = c * r
            ph_ref[h, lo:hi, :] = ph
            rp_ref[h, lo:hi, :] = jnp.broadcast_to(r, ph.shape)
            outs.append(q[h].astype(f32) + ph * g_ref[h] + b_ref[h])
        out_ref[lo:hi, :] = jnp.concatenate(outs, axis=1)
    out = out_ref[...]
    gate = gate_ref[...]
    gated = (gate * normal_parts(gate)[0] * out).astype(bf16)
    for p, ref in enumerate((p0_ref, p1_ref, p2_ref, p3_ref)):
        @pl.when(which == p)
        def _(ref=ref):
            ref[...] = gated


FWD_NAMES = ("p0", "p1", "p2", "p3", "out", "gate", "norm", "qkv", "eb", "er", "a", "gp", "hg", "g1", "g2", "w2all", "w1c", "c1c", "c2c",
             "zh", "eg", "va", "vb", "vd", "vr", "bq", "gq", "ph", "rp")


def ttt_forward(order, pieces, gain, w_proj, w_wide, b_wide, w_tall, b_tall, w1, c1, w2t, c2, g, b):
    nh, hd, inner = w1.shape
    n = order.shape[1]
    rows_here, width = pieces[0].shape
    L = 4 * rows_here
    C = L // n
    per = C // MB
    span = nh * hd
    sd = jax.ShapeDtypeStruct
    full = lambda *s: pl.BlockSpec(s, lambda i, order: (0,) * len(s))
    tok = lambda w: pl.BlockSpec((nh, C, w), lambda i, order: (0, i, 0))
    lead = lambda *s: pl.BlockSpec(s, lambda i, order: (i,) + (0,) * (len(s) - 1))
    flat = lambda w, row: pl.BlockSpec((C, w), lambda i, order: (order[row, i], 0))
    big = (sd((nh, L, inner), bf16), tok(inner))
    small = (sd((nh, L, hd), f32), tok(hd))
    outs = [(sd((rows_here, span), bf16), flat(span, 5 + p)) for p in range(4)]
    outs += [(sd((L, span), f32), flat(span, 3)), (sd((L, span), f32), flat(span, 3)), (sd((L, width), bf16), flat(width, 3)),
             (sd((L, 3 * span), bf16), lead(C, 3 * span)), (sd((nh, L, 128), f32), tok(128)),
             (sd((8, L), f32), pl.BlockSpec((8, C), lambda i, order: (0, i))),
             big, big, big, big, (sd((nh, L, hd), bf16), tok(hd)),
             (sd((L // MB, nh, hd, inner), bf16), lead(per, nh, hd, inner)),
             (sd((n, nh, hd, inner), bf16), lead(1, nh, hd, inner)),
             (sd((n, nh, 1, inner), f32), lead(1, nh, 1, inner)),
             (sd((n, nh, 1, hd), f32), lead(1, nh, 1, hd)),
             small, small, small, small, small, small, big, big, small, small]
    args = (gain, w_proj, w_wide, b_wide, w_tall, b_tall, w1, c1, w2t, c2, g, b)
    res = pl.pallas_call(
        functools.partial(fwd_kernel, nh),
        grid_spec=pltpu.PrefetchScalarGridSpec(
            num_scalar_prefetch=1, grid=(n,),
            in_specs=[flat(width, 5 + p) for p in range(4)] + [full(*x.shape) for x in args],
            out_specs=[o[1] for o in outs],
            scratch_shapes=[pltpu.VMEM((nh, hd, inner), f32), pltpu.VMEM((nh, hd, inner), f32), pltpu.VMEM((nh, 1, inner), f32),
                            pltpu.VMEM((nh, 1, hd), f32), pltpu.VMEM((nh, C, hd), bf16), pltpu.VMEM((nh, C, hd), bf16),
                            pltpu.VMEM((nh, C, hd), f32), pltpu.VMEM((nh, C, inner), f32), pltpu.VMEM((nh, BODY, inner), f32),
                            pltpu.VMEM((nh, C, inner), bf16), pltpu.VMEM((C, 4 * span), f32), pltpu.VMEM((C, width), bf16),
                            pltpu.VMEM((nh, C, hd), f32)]),
        out_shape=[o[0] for o in outs],
        compiler_params=pltpu.CompilerParams(vmem_limit_bytes=VMEM_BYTES),
        cost_estimate=pl.CostEstimate(flops=10**11, bytes_accessed=10**8, transcendentals=0),
        name="ttt_forward",
    )(order, *pieces, *args)
    return dict(zip(FWD_NAMES, res))


def bwd_kernel(nh, order_ref, da_ref, db_half_ref, qkv_ref, eb_ref, etar_ref, g_ref, b_ref, a_ref, gp_ref, hg_ref, g1_ref, g2_ref, w2all_ref, w1c_ref,
               zh_ref, eg_ref, va_ref, vb_ref, vd_ref, vr_ref, bq_ref, gq_ref, ph_ref, rp_ref,
               dqkv_ref, state_ref, small_ref,
               d1_s, d2_s, e1_s, e2_s, k_s, pa_s, pg1_s, pg2_s, z1_s, u_s, y_s, pre_s, cur_s, dt_ref, dg_ref, db_ref, br_s, n1_s, n2_s, s1_s, s2_s, p1_s, p2_s, dk_s, drow_s):
    hd = d1_s.shape[1]
    inner = d1_s.shape[2]
    C = qkv_ref.shape[0]
    H = range(nh)
    inv = 1.0 / hd

    @pl.when(pl.program_id(0) == 0)
    def _():
        for ref in (d1_s, d2_s, e1_s, e2_s, dg_ref, db_ref, br_s, n1_s, n2_s, s1_s, s2_s, p1_s, p2_s, dk_s, drow_s):
            ref[...] = jnp.zeros_like(ref)

    near = order_ref[0, pl.num_programs(0) - 1 - pl.program_id(0)] == 0

    @pl.when(near)
    def _():
        dt_ref[...] = da_ref[...]

    @pl.when(jnp.logical_not(near))
    def _():
        dt_ref[...] = db_half_ref[...]

    ends = []
    for h in H:
        k_s[h] = qkv_ref[:, (nh + h) * hd:(nh + h + 1) * hd]
        ends.append((d1_s[h].astype(bf16), e1_s[h]))
    drow_s[...] = jnp.zeros_like(drow_s)
    for lo in range(0, C, TILE):
        hi = lo + TILE
        here = slice(lo, hi)
        tri = lax.broadcasted_iota(jnp.int32, (TILE, hi), 0) + lo >= lax.broadcasted_iota(jnp.int32, (TILE, hi), 1)
        q = [qkv_ref[here, h * hd:(h + 1) * hd] for h in H]
        M = [jnp.where(tri, etar_ref[h:h + 1, :hi], 0.0) for h in H]
        dO, dP2 = [], []
        for h in H:
            d = dt_ref[here, h * hd:(h + 1) * hd]
            ph = ph_ref[h, here, :]
            dg_ref[h] += jnp.sum(d * ph, axis=0, keepdims=True)
            db_ref[h] += jnp.sum(d, axis=0, keepdims=True)
            x = d * g_ref[h]
            p = (rp_ref[h, here, :] * (x - rows(x) * inv - ph * (rows(x * ph) * inv))).astype(bf16)
            dO.append(d)
            dP2.append(p)
            p2_s[h, here, :] = p
        N2 = [M[h] * (nt(bq_ref[h, here, :], a_ref[h, :hi, :]) + 1.0) for h in H]
        dN2 = [nt(dP2[h], g2_ref[h, :hi, :]) for h in H]
        dS2 = [(dN2[h] * M[h]).astype(bf16) for h in H]
        for h in H:
            n2_s[h, here, :hi] = N2[h].astype(bf16)
            s2_s[h, here, :hi] = dS2[h]
            drow_s[h:h + 1, :hi] -= jnp.sum(dN2[h] * N2[h], axis=0, keepdims=True)
        dP1 = []
        for h in H:
            dB = nn(dP2[h], w2all_ref[0, h]) - nn(dS2[h], a_ref[h, :hi, :])
            dP1.append((dB * gq_ref[h, here, :].astype(f32)).astype(bf16))
            p1_s[h, here, :] = dP1[h]
        N1 = [M[h] * (nt(q[h], k_s[h, :hi, :]) + 1.0) for h in H]
        dN1 = [nt(dP1[h], g1_ref[h, :hi, :]) for h in H]
        dS1 = [(dN1[h] * M[h]).astype(bf16) for h in H]
        for h in H:
            n1_s[h, here, :hi] = N1[h].astype(bf16)
            s1_s[h, here, :hi] = dS1[h]
            drow_s[h:h + 1, :hi] -= jnp.sum(dN1[h] * N1[h], axis=0, keepdims=True)
        dq = [(dO[h] + nt(dP1[h], w1c_ref[0, h]) - nn(dS1[h], k_s[h, :hi, :])).astype(bf16) for h in H]
        dqkv_ref[here, :nh * hd] = jnp.concatenate(dq, axis=1)
    for lo in range(0, C, WIDE):
        cols = slice(lo, lo + WIDE)
        for h in H:
            pa_s[h, cols, :] = -tn(s2_s[h, lo:, cols], bq_ref[h, lo:, :])
            pg2_s[h, cols, :] = -tn(n2_s[h, lo:, cols], p2_s[h, lo:, :])
            pg1_s[h, cols, :] = -tn(n1_s[h, lo:, cols], p1_s[h, lo:, :])
            dk_s[h, cols, :] = -tn(s1_s[h, lo:, cols], qkv_ref[lo:, h * hd:(h + 1) * hd])
    steps = SPAN // MB
    bodies = C // SPAN
    for h in H:
        pre_s[h] = nn(k_s[h], ends[h][0]) + ends[h][1]
    D2 = [d2_s[h] for h in H]
    e2 = [e2_s[h] for h in H]
    esum = [jnp.zeros((MB, hd), f32) for h in H]
    gsum = [jnp.zeros((MB, hd), f32) for h in H]
    zsum = [jnp.zeros((MB, inner), f32) for h in H]
    for j in reversed(range(bodies)):
        lo, hi = j * SPAN, (j + 1) * SPAN
        kb = [k_s[h, lo:hi, :] for h in H]
        mix = [(nt(kb[h], kb[h]) + 1.0).astype(bf16) for h in H]
        for h in H:
            if hi < C:
                later = (nt(kb[h], k_s[h, hi:, :]) + 1.0).astype(bf16)
                cur_s[h] = pre_s[h, lo:hi, :] + nn(later, z1_s[h, hi:, :])
            else:
                cur_s[h] = pre_s[h, lo:hi, :]
        dz = [[] for h in H]
        for u in reversed(range(steps)):
            i = j * steps + u
            sl = slice(i * MB, (i + 1) * MB)
            e = [eb_ref[h, sl, :] for h in H]
            ew = [jnp.concatenate([e[h]] * (inner // 128), axis=1) for h in H]
            en = [e[h][:, :hd] for h in H]
            D2b = [D2[h].astype(bf16) for h in H]
            a = [a_ref[h, sl, :] for h in H]
            G2 = [g2_ref[h, sl, :] for h in H]
            w2 = [w2all_ref[i, h] for h in H]
            gp = [gp_ref[h, sl, :].astype(f32) for h in H]
            y1 = [cur_s[h, u * MB:(u + 1) * MB, :] for h in H]
            if u < steps - 1:
                fill = jnp.zeros(((u + 1) * MB, inner), bf16)
                y1 = [y1[h] + nn(mix[h][u * MB:(u + 1) * MB], jnp.concatenate([fill] + dz[h], axis=0)) for h in H]
            y2 = [nt(a[h], D2b[h]) + e2[h] for h in H]
            dG1 = [pg1_s[h, sl, :] - ew[h] * y1[h] for h in H]
            dH = [(dG1[h] * gp[h]).astype(bf16) for h in H]
            U = [pg2_s[h, sl, :] - en[h] * y2[h] + nt(dH[h], w2[h]) for h in H]
            dAp = [pa_s[h, sl, :] - ew[h] * nn(G2[h], D2b[h]) for h in H]
            dZb, dAz = [], []
            for h in H:
                vw = nn(jnp.concatenate([vb_ref[h, sl, :], vd_ref[h, sl, :]], axis=0), w2[h])
                uva = U[h] * va_ref[h, sl, :]
                main = nn(uva, w2[h])
                uu = U[h]
                zh, eg = zh_ref[h, sl, :], eg_ref[h, sl, :]
                u1 = rows(uu * zh) * inv
                ue = rows(uu * eg) * inv
                ua = rows(uva) * inv
                dZ = uva - u1 * vb_ref[h, sl, :] - ue * vd_ref[h, sl, :] - ua
                dZb.append(dZ.astype(bf16))
                dAz.append(main - u1 * vw[:MB] - ue * vw[MB:])
                dE = vr_ref[h, sl, :] * (uu - rows(uu) * inv - zh * u1)
                u_s[h, sl, :] = dE
                esum[h] = esum[h] + dE
                gsum[h] = gsum[h] + dE * eg
                y_s[h, sl, :] = G2[h].astype(f32) * y2[h]
            for h in H:
                dZ1 = (dAp[h] + dAz[h]) * gp[h] + dG1[h] * hg_ref[h, sl, :].astype(f32)
                z = dZ1.astype(bf16)
                dz[h].insert(0, z)
                z1_s[h, sl, :] = z
                zsum[h] = zsum[h] + dZ1
                D2[h] = D2[h] + tn(jnp.concatenate([dZb[h], G2[h]], axis=0), jnp.concatenate([a[h], dH[h]], axis=0))
                e2[h] = e2[h] + jnp.sum(dZb[h].astype(f32), axis=0, keepdims=True)
    for h in H:
        d1_s[h] = d1_s[h] + tn(k_s[h], z1_s[h])
        e1_s[h] = e1_s[h] + jnp.sum(zsum[h], axis=0, keepdims=True)
        d2_s[h] = D2[h]
        e2_s[h] = e2[h]

    ones = jnp.ones((C, hd), f32)
    only = (lax.broadcasted_iota(jnp.int32, (C, hd), 1) == 0).astype(f32)
    for lo in range(0, C, TILE):
        hi = lo + TILE
        here = slice(lo, hi)
        blk = (lax.broadcasted_iota(jnp.int32, (TILE, hi), 0) + lo) // MB > lax.broadcasted_iota(jnp.int32, (TILE, hi), 1) // MB
        X = [jnp.where(blk, nt(z1_s[h, here, :], g1_ref[h, :hi, :]), 0.0).astype(bf16) for h in H]
        for h in H:
            s1_s[h, here, :hi] = X[h]
            ek = eb_ref[h, :hi, :hd] * k_s[h, :hi, :].astype(f32)
            dk_s[h, here, :] += nt(z1_s[h, here, :], w1c_ref[0, h]) - nn(X[h], ek)
    dks, dvs, dcol = [], [], []
    for h in H:
        k = k_s[h].astype(f32)
        g = g_ref[h]
        e = eb_ref[h, :, :hd]
        D1e, d1e = ends[h]
        wide_k = jnp.concatenate([k, ones], axis=1).astype(bf16)
        R = nt(g1_ref[h], jnp.concatenate([D1e, jnp.broadcast_to(d1e, D1e.shape).astype(bf16)], axis=0))
        R = R + jnp.concatenate([tn(s1_s[h, lo:, lo:lo + WIDE], wide_k[lo:]) for lo in range(0, C, WIDE)], axis=0)
        dcol.append(-e[:, :1] * (rows(R * jnp.concatenate([k, only], axis=1)) + rows(y_s[h])) * (1.0 - e[:, :1] * (hd / base_rate)))
        dv = u_s[h] * g
        db_ref[h] += jnp.sum(esum[h], axis=0, keepdims=True) * g
        dg_ref[h] += jnp.sum(gsum[h], axis=0, keepdims=True) / g
        dks.append((dk_s[h] - e * R[:, :hd] + dv).astype(bf16))
        dvs.append((-dv).astype(bf16))
        q = qkv_ref[:, h * hd:(h + 1) * hd]
        d1_s[h] += tn(q, p1_s[h])
        d2_s[h] += tn(p2_s[h], bq_ref[h])
        e1_s[h] += jnp.sum(p1_s[h].astype(f32), axis=0, keepdims=True)
        e2_s[h] += jnp.sum(p2_s[h].astype(f32), axis=0, keepdims=True)
    drow = drow_s[...] * (1.0 - etar_ref[...] * (hd / base_rate))
    turned = drow.T
    drate = [(dcol[h] + turned[:, h:h + 1]).astype(bf16) for h in H]
    for h in H:
        br_s[h] += jnp.broadcast_to(jnp.sum(drate[h].astype(f32), axis=0, keepdims=True), (1, hd))
    fill = jnp.zeros((C, dqkv_ref.shape[1] - 3 * nh * hd - nh), bf16)
    dqkv_ref[:, nh * hd:] = jnp.concatenate(dks + dvs + drate + [fill], axis=1)

    @pl.when(pl.program_id(0) == pl.num_programs(0) - 1)
    def _():
        small = [e1_s[h] for h in H] + [jnp.concatenate([e2_s[h], dg_ref[h], db_ref[h], br_s[h]], axis=1) for h in H]
        small_ref[...] = jnp.concatenate(small + [jnp.zeros((8 - 2 * nh, inner), f32)], axis=0)
        for i in range(inner // 128):
            for j, ref in enumerate((d1_s, d2_s)):
                for h in H:
                    at = ((2 * i + j) * nh + h) * hd
                    state_ref[at:at + hd, :] = ref[h, :, i * 128:(i + 1) * 128].astype(bf16)


def ttt_backward(order, dt, g, b, o):
    n = order.shape[1]
    L = 2 * dt[0].shape[0]
    C = L // n
    nh, hd, inner = o["w1c"].shape[1:]
    per = C // MB
    span = nh * hd
    wide = -(-(3 * span + nh) // 128) * 128
    sd = jax.ShapeDtypeStruct
    full = lambda *s: pl.BlockSpec(s, lambda i, order: (0,) * len(s))
    tok = lambda w: pl.BlockSpec((nh, C, w), lambda i, order: (0, n - 1 - i, 0))
    flat = lambda w, row: pl.BlockSpec((C, w), lambda i, order: (order[row, n - 1 - i], 0))
    lead = lambda *s: pl.BlockSpec(s, lambda i, order: (n - 1 - i,) + (0,) * (len(s) - 1))
    big, small = tok(inner), tok(hd)
    names = ("a", "gp", "hg", "g1", "g2", "w2all", "w1c", "zh", "eg", "va", "vb", "vd", "vr", "bq", "gq", "ph", "rp")
    specs = [big, big, big, big, small, lead(per, nh, hd, inner), lead(1, nh, hd, inner),
             small, small, small, small, small, small, big, big, small, small]
    state = 2 * span * inner // 128
    return pl.pallas_call(
        functools.partial(bwd_kernel, nh),
        grid_spec=pltpu.PrefetchScalarGridSpec(
            num_scalar_prefetch=1, grid=(n,),
            in_specs=[flat(span, 1), flat(span, 2), lead(C, 3 * span), tok(128), pl.BlockSpec((8, C), lambda i, order: (0, n - 1 - i)),
                      full(nh, 1, hd), full(nh, 1, hd)] + specs,
            out_specs=[flat(wide, 3), full(state, 128), full(8, inner)],
            scratch_shapes=[pltpu.VMEM((nh, hd, inner), f32), pltpu.VMEM((nh, hd, inner), f32), pltpu.VMEM((nh, 1, inner), f32),
                            pltpu.VMEM((nh, 1, hd), f32), pltpu.VMEM((nh, C, hd), bf16), pltpu.VMEM((nh, C, inner), f32),
                            pltpu.VMEM((nh, C, inner), f32), pltpu.VMEM((nh, C, hd), f32), pltpu.VMEM((nh, C, inner), bf16),
                            pltpu.VMEM((nh, C, hd), f32), pltpu.VMEM((nh, C, hd), f32), pltpu.VMEM((nh, C, inner), f32),
                            pltpu.VMEM((nh, SPAN, inner), f32), pltpu.VMEM((C, span), f32), pltpu.VMEM((nh, 1, hd), f32),
                            pltpu.VMEM((nh, 1, hd), f32), pltpu.VMEM((nh, 1, hd), f32)]
            + [pltpu.VMEM((nh, C, C), bf16)] * 4
            + [pltpu.VMEM((nh, C, inner), bf16), pltpu.VMEM((nh, C, hd), bf16), pltpu.VMEM((nh, C, hd), f32), pltpu.VMEM((8, C), f32)]),
        out_shape=[sd((L, wide), bf16), sd((state, 128), bf16), sd((8, inner), f32)],
        compiler_params=pltpu.CompilerParams(vmem_limit_bytes=VMEM_BYTES),
        cost_estimate=pl.CostEstimate(flops=13 * 10**10, bytes_accessed=10**8, transcendentals=0),
        name="ttt_backward",
    )(order, *dt, o["qkv"], o["eb"], o["er"], g, b, *[o[k] for k in names])


def pack_kernel(nh, grad_ref, w_ref, cols_ref, state_ref, small_ref, out_ref):
    used = grad_ref.shape[1]
    per = small_ref.shape[1]
    turned = small_ref[...].T
    dots = rows(grad_ref[...] * w_ref[...].astype(f32)) + cols_ref[:, :1]
    out_ref[:, :used - 128] = grad_ref[:, :used - 128].astype(bf16)
    lane = lax.broadcasted_iota(jnp.int32, (per, 128), 1)
    for h in range(nh):
        here = slice(h * per, (h + 1) * per)
        tile = grad_ref[here, used - 128:]
        for i, col in enumerate((dots[here], cols_ref[here, 1:2], turned[:, h:h + 1], turned[:, nh + h:nh + h + 1])):
            tile = jnp.where(lane == 127 - i, col, tile)
        out_ref[here, used - 128:used] = tile.astype(bf16)
    out_ref[:, used:] = state_ref[...]


def pack(grad, w, cols, state, small, nh):
    spec = pl.BlockSpec(memory_space=pltpu.VMEM)
    return pl.pallas_call(
        functools.partial(pack_kernel, nh), in_specs=[spec] * 5, out_specs=spec,
        out_shape=jax.ShapeDtypeStruct((grad.shape[0], grad.shape[1] + 128), bf16),
        compiler_params=pltpu.CompilerParams(vmem_limit_bytes=VMEM_BYTES), name="pack",
    )(grad, w, cols, state, small)


def unpack_kernel(nh, hd, inner, ctx_ref, own_ref, side_ref, qkv_ref, rate_ref, w1_ref, w2_ref, c1_ref, c2_ref, ig_ref, ib_ref, br_ref, gains_ref):
    span = nh * hd
    used = own_ref.shape[1] - 128
    first = ctx_ref[0] == 0
    total = 0.0
    for part, (one, two) in enumerate(((own_ref, side_ref), (side_ref, own_ref))):
        def take(rows_at, lanes_at):
            return jnp.where(first, one[rows_at, lanes_at], two[rows_at, lanes_at]).astype(f32)

        every = slice(None)
        body = take(every, slice(0, used))
        for i in range(3):
            qkv_ref[i, :, part * span:(part + 1) * span] = body[:, i * span:(i + 1) * span]
        turned = body[:, used - 128:].T
        at = 3 * span - (used - 128)
        rate_ref[part * nh:(part + 1) * nh, :] = turned[at:at + nh]
        total = total + turned[126:128]
        for h in range(nh):
            at = part * nh + h
            c1_ref[at:at + 1, :] = turned[125:126, h * inner:(h + 1) * inner]
            for i, ref in enumerate((c2_ref, ig_ref, ib_ref, br_ref)):
                ref[at:at + 1, :] = turned[124:125, h * inner + i * hd:h * inner + (i + 1) * hd]
            for j in range(2):
                w = jnp.concatenate([take(slice(((2 * i + j) * nh + h) * hd, ((2 * i + j) * nh + h + 1) * hd), slice(used, used + 128))
                                     for i in range(inner // 128)], axis=1)
                if j == 0:
                    w1_ref[at] = w
                else:
                    w2_ref[at] = w - jnp.sum(w, axis=0, keepdims=True) * (1.0 / hd)
    gains_ref[...] = total
    c2_ref[...] = c2_ref[...] - rows(c2_ref[...]) * (1.0 / hd)


def unpack(ctx, own, side, nh, hd, inner):
    spec = pl.BlockSpec(memory_space=pltpu.VMEM)
    rows_all = own.shape[0]
    shapes = [(3, rows_all, 2 * nh * hd), (2 * nh, rows_all), (2 * nh, hd, inner), (2 * nh, hd, inner), (2 * nh, inner), (2 * nh, hd),
              (2 * nh, hd), (2 * nh, hd), (2 * nh, hd), (2, rows_all)]
    found = pl.pallas_call(
        functools.partial(unpack_kernel, nh, hd, inner),
        in_specs=[pl.BlockSpec(memory_space=pltpu.SMEM), spec, spec], out_specs=[spec] * len(shapes),
        out_shape=[jax.ShapeDtypeStruct(s, f32) for s in shapes],
        compiler_params=pltpu.CompilerParams(vmem_limit_bytes=VMEM_BYTES), name="unpack",
    )(ctx, own, side)
    return (jnp.swapaxes(found[0], 0, 1), found[1].T, found[2], jnp.swapaxes(found[3], 1, 2)) + tuple(found[4:])


def swap(value, axis):
    count = lax.axis_size(axis)
    return lax.ppermute(value, axis, [(i, (i + 1) % count) for i in range(count)])


def matmul(left_op, right_op):
    return jnp.dot(left_op, right_op, preferred_element_type=f32)


def matmul_nt(left_op, right_op):
    return lax.dot_general(left_op, right_op, (((1,), (1,)), ((), ())), preferred_element_type=f32)


def matmul_tn(left_op, right_op):
    return lax.dot_general(left_op, right_op, (((0,), (0,)), ((), ())), preferred_element_type=f32)


def gelu_value(values):
    return 0.5 * values * (1.0 + lax.erf(values * 0.7071067811865476))


def gelu_slope(values):
    return 0.5 * (1.0 + lax.erf(values * 0.7071067811865476)) + values * jnp.exp(-0.5 * values * values) * 0.3989422804014327


def rms_gain(values, gains):
    return values * lax.rsqrt(jnp.mean(values * values, axis=-1, keepdims=True) + 1e-06) * gains


def local(tokens, upstream, group_ids, group_weights, norm_gain1, w_qkv, w_gate, w_rate, b_rate, w1_init, c1_init, w2_init,
          c2_init, inner_gain, inner_bias, out_proj, norm_gain2, w_gu, w_down):
    _, _, rows_here, width = tokens.shape
    chains = w1_init.shape[0] // lax.axis_size("ctx")
    head_dim, inner = w1_init.shape[1:]
    span = chains * head_dim
    ff = w_down.shape[0]
    half = 2 * rows_here
    ctx, head = lax.axis_index("ctx"), lax.axis_index("head")
    together = lax.optimization_barrier

    def diag(value):
        return lax.ppermute(value, ("head", "ctx"), [(i, 3 - i) for i in range(4)])

    def mine(array, axis, size, at=ctx):
        return lax.dynamic_slice_in_dim(array, at * size, size, axis)

    per = rows_here // CHUNK
    chunk = jnp.arange(4 * per, dtype=jnp.int32)
    quarter, inside = chunk // per, chunk % per
    here = (2 * ctx + head).astype(jnp.int32)
    is_far = (quarter ^ here) & 1
    slot = (quarter ^ here) >> 1
    near_at = jnp.clip(chunk - 2 * per * (quarter >> 1) - per * (here & 1), 0, per - 1) + slot * per
    far_at = jnp.clip(chunk - 2 * per * (quarter >> 1) - per * (1 - (here & 1)), 0, per - 1) + slot * per
    at_piece = [jnp.clip(chunk - (here ^ mask) * per, 0, per - 1) for mask in (0, 2, 1, 3)]
    order = jnp.stack([is_far, near_at, far_at, is_far * 2 * per + slot * per + inside, 2 * is_far + slot] + at_piece)

    own = tokens.reshape(rows_here, width)
    across = swap(own, "head")
    pieces = (own, swap(own, "ctx"), across, swap(across, "ctx"))
    w_qkv_here = mine(w_qkv, 2, span).reshape(width, 3 * span)
    w_gate_here = mine(w_gate, 1, span)
    w_rate_here, b_rate_here = mine(w_rate, 1, chains), mine(b_rate, 0, chains)
    w_proj = jnp.concatenate([w_qkv_here, w_gate_here], axis=1)
    w_wide, b_wide = jnp.repeat(w_rate_here, 128, axis=1), jnp.repeat(b_rate_here, 128)[None]
    w_tall = jnp.pad(w_rate_here.T, ((0, 8 - chains), (0, 0)))
    b_tall = jnp.broadcast_to(jnp.pad(b_rate_here, (0, 8 - chains))[:, None], (8, 128))
    w_ext = jnp.pad(jnp.concatenate([w_qkv_here, w_rate_here], axis=1), ((0, 0), (0, -(3 * span + chains) % 128)))
    w1, w2 = mine(w1_init, 0, chains), mine(w2_init, 0, chains)
    c1, c2 = mine(c1_init, 0, chains), mine(c2_init, 0, chains)
    gain, bias = mine(inner_gain, 0, chains)[:, None], mine(inner_bias, 0, chains)[:, None]
    w2_mid = jnp.swapaxes(w2 - jnp.mean(w2, axis=2, keepdims=True), 1, 2)
    c2_mid = (c2 - jnp.mean(c2, axis=1, keepdims=True))[:, None]
    kept = ttt_forward(order, pieces, norm_gain1[None], w_proj, w_wide, b_wide, w_tall, b_tall, w1, c1[:, None], w2_mid, c2_mid, gain, bias)
    cot = upstream.reshape(rows_here, width)
    gated0, cot_across, proj_far = together((kept["p0"], swap(cot, "head"), swap(out_proj, "head")))
    gated = (gated0, kept["p1"], kept["p2"], kept["p3"])
    residual = own.astype(f32)
    normed_all, ttt_out, gate_pre = kept["norm"], kept["out"], kept["gate"]

    def own_first(array, axis):
        size = array.shape[axis] // 2
        return jnp.concatenate([mine(array, axis, size), mine(array, axis, size, 1 - ctx)], axis=axis)

    w_out = jnp.concatenate([own_first(out_proj, 0), own_first(proj_far, 0)], axis=0)
    cols_far = [gated[2], swap(gated[3], "ctx"), swap(gated[0], "head"), diag(gated[1])]
    cols_own = [gated[0], swap(gated[1], "ctx"), swap(gated[2], "head"), diag(gated[3])]
    chip_cols = jnp.concatenate([jnp.concatenate(cols_own[:2], axis=1), jnp.concatenate(cols_far[:2], axis=1)], axis=0)
    group_count = group_weights.shape[0]
    picked = jnp.sum(jnp.where(group_ids[0] == jnp.arange(group_count, dtype=jnp.int32), group_weights, 0)).astype(f32)
    cotangent = cot.astype(f32) * picked
    cot_own, cot_far = cotangent.astype(bf16), (cot_across.astype(f32) * picked).astype(bf16)
    w_gu_flat = w_gu.reshape(width, 2 * ff)

    def out_rows(start, cols):
        middle = start + matmul(jnp.concatenate(cols, axis=1), w_out)
        return middle, rms_gain(middle, norm_gain2).astype(bf16)

    def feed_forward(normed_rows, cot_rows):
        gate_up = matmul(normed_rows, w_gu_flat)
        gate_part, up_part = gate_up[:, :ff], gate_up[:, ff:]
        sig = jax.nn.sigmoid(gate_part)
        silu = gate_part * sig
        hidden = (silu * up_part).astype(bf16)
        d_hidden = matmul_nt(cot_rows, w_down)
        d_gate = d_hidden * up_part * (sig + silu * (1.0 - sig))
        d_gate_up = jnp.concatenate([d_gate, d_hidden * silu], axis=1).astype(bf16)
        return hidden, d_gate_up, matmul_nt(d_gate_up, w_gu_flat)

    _, two_far = out_rows(across.astype(f32), cols_far)
    hidden_far, d_gu_far, input_far = feed_forward(two_far, cot_far)
    input_met = swap(input_far.astype(bf16), "head")
    input_far, cols_own[0] = together((input_far, cols_own[0]))
    middle, two_own = out_rows(residual, cols_own)
    hidden, d_gu, input_own = feed_forward(two_own, cot_own)
    grad_down = (matmul_tn(hidden, cot_own) + matmul_tn(hidden_far, cot_far)).astype(bf16)
    grad_gu = (matmul_tn(two_own, d_gu) + matmul_tn(two_far, d_gu_far)).astype(bf16)
    input_met, input_own, grad_down, grad_gu = together((input_met, input_own, grad_down, grad_gu))
    d_normed_two = input_own + input_met.astype(f32)
    _, norm_back_two = jax.vjp(rms_gain, middle, norm_gain2)
    d_middle_norm, grad_gain2 = norm_back_two(d_normed_two)
    d_middle = cotangent + d_middle_norm

    d_low = d_middle.astype(bf16)
    d_across = swap(d_low, "head")
    proj_here = w_out[:span]

    def gate_back(d_rows, at):
        d_gated, pre = matmul_nt(d_rows, proj_here), gate_pre[at]
        return d_gated * gelu_value(pre), (d_gated * ttt_out[at] * gelu_slope(pre)).astype(bf16)

    d_ttt_near, d_gate_near = gate_back(jnp.concatenate([d_low, swap(d_low, "ctx")], axis=0), slice(0, half))
    terms_far = matmul(hidden_far, w_down).astype(bf16)
    terms_own = middle + matmul(hidden, w_down)
    d_across, d_ttt_near, d_gate_near, terms_far, terms_own = together((d_across, d_ttt_near, d_gate_near, terms_far, terms_own))
    d_ttt_far, d_gate_far = gate_back(jnp.concatenate([d_across, swap(d_across, "ctx")], axis=0), slice(half, 2 * half))
    grad_out = matmul_tn(chip_cols, jnp.concatenate([d_low, d_across], axis=0))
    grad_out = jnp.where(ctx == 0, grad_out, jnp.concatenate([grad_out[span:], grad_out[:span]], axis=0)).astype(bf16)
    grad_gate = matmul_tn(normed_all[:half], d_gate_near) + matmul_tn(normed_all[half:], d_gate_far)
    dot_gate = jnp.sum(grad_gate * w_gate_here.astype(f32), axis=1)
    grad_gate = grad_gate.astype(bf16)
    zero = jnp.zeros_like(grad_gate)
    grad_gate = jnp.concatenate([jnp.where(ctx == 0, grad_gate, zero), jnp.where(ctx == 0, zero, grad_gate)], axis=1)
    grad_down, grad_gu, grad_out, grad_gate, d_ttt_near = together((grad_down, grad_gu, grad_out, grad_gate, d_ttt_near))
    early = lax.psum((grad_down, grad_gu, grad_out, grad_gate), ("dp", "ctx"))
    terms_met = swap(terms_far, "head")
    d_ext, state, small = ttt_backward(order, (d_ttt_near, d_ttt_far), gain, bias, kept)
    d_ext, terms_met = together((d_ext, terms_met))
    output = (terms_own + terms_met.astype(f32)).astype(bf16)

    message = pack(matmul_tn(normed_all, d_ext), w_ext, jnp.stack([dot_gate, grad_gain2], axis=1), state, small, chains)
    count = lax.axis_size("dp")
    slab = message.shape[0] // count
    parts = lax.all_to_all(message, "dp", 0, 0, tiled=True)

    early, d_rest = together((early, d_ext))
    terms_near = matmul_nt(d_rest[:half], w_ext) + matmul_nt(d_gate_near, w_gate_here)
    terms_far = matmul_nt(d_rest[half:], w_ext) + matmul_nt(d_gate_far, w_gate_here)
    given = swap(jnp.concatenate([terms_near[rows_here:], terms_far[rows_here:]], axis=0).astype(bf16), "ctx").astype(f32)
    d_one = terms_near[:rows_here] + given[:rows_here]
    send = (terms_far[:rows_here] + given[rows_here:]).astype(bf16)
    send, d_one, parts = together((send, d_one, parts))
    d_one_met = swap(send, "head")
    grad_down, grad_gu, grad_out, grad_gate = [part.astype(f32) for part in early]
    grad_gu = grad_gu.reshape(w_gu.shape)
    total = jnp.sum(parts.reshape(count, slab, message.shape[1]).astype(f32), axis=0).astype(bf16)
    late = lax.all_to_all(jnp.broadcast_to(total[None], (count,) + total.shape), "dp", 0, 0, tiled=True).reshape(message.shape)
    d_normed_one = d_one + d_one_met.astype(f32)
    _, norm_back_one = jax.vjp(rms_gain, residual, norm_gain1)
    x_grad = d_middle + norm_back_one(d_normed_one)[0]
    late, x_grad, grad_down, grad_gu, grad_out, grad_gate, output = together((late, x_grad, grad_down, grad_gu, grad_out, grad_gate, output))
    (grad_qkv, grad_rate, grad_w1, grad_w2, grad_c1, grad_c2, grad_igain, grad_ibias, grad_brate, gains) = unpack(
        ctx.astype(jnp.int32)[None], late, swap(late, "ctx"), chains, head_dim, inner)
    gains = gains + swap(gains, "head")
    return (output.reshape(tokens.shape), x_grad.reshape(tokens.shape), gains[1] / norm_gain1, grad_qkv, grad_gate, grad_rate,
            grad_brate[:, 0], grad_w1, grad_c1, grad_w2, grad_c2, grad_igain, grad_ibias, grad_out, gains[0], grad_gu, grad_down)


def solution(mesh):
    rows = P("dp", "ctx", "head", None)
    split = P("head", None)
    cube = P("head", None, None)
    last = P(None, "head")
    deep = P(None, None, "head")
    in_specs = (rows, rows, P("dp"), P(), P(), deep, last, last, P("head"), cube, split, cube, split, split, split, split, P(), deep, split)
    out_specs = (rows, rows, P(), deep, last, last, P("head"), cube, split, cube, split, split, split, split, P(), deep, split)
    return jax.shard_map(local, mesh=mesh, in_specs=in_specs, out_specs=out_specs, check_vma=False)
```
